256 devices in a mesh: depth: 4 (over y), row: 16 (over z, core), col: 4 (over x).
Axes of the slice: x: 4, y: 4, z: 8, core: 2. Of those that a mesh axis runs over, the one named last changes fastest.
Arguments:
- field: float32 [128, 2048, 2048], P('depth', 'row', 'col'), may hold values from 0.1 to 10
- view_order: int32 [4], replicated, may hold values from 0 to 3, each once
Outputs:
- image: float32 [4, 2048, 2048], P('depth', 'row', 'col')
The draws below stay inside these ranges and needn't reach their ends.
Inputs may be any that keep to these rules, and one draw needn't show every extreme that they name: `view_order`: each brick index appears exactly once.
All inputs are finite; a program needn't handle non-finite values.
Results may differ from the reference program's by a relative error of at most 0.0003.
Values sent between devices are 32-bit elements; how exact they have to be, the bound alone decides.
A program may use at most 192 MiB of HBM per device.

```python
import math
import jax
import jax.numpy as jnp
from jax import lax

CZ = 32
NZ = 128
NY = 2048
NX = 2048
N_DEPTH = 4


def block_scale(rng, dims, shards, low, high):
    def one(dim, parts):
        steps = jax.random.uniform(jax.random.fold_in(jax.random.fold_in(rng, 6), dim), (parts,), jnp.float32, low / len(shards), high / len(shards))
        return jnp.repeat(jnp.exp(steps), dims[dim] // parts).reshape((-1,) + (1,) * (len(dims) - dim - 1))

    loudness = one(*shards[0])
    for cut in shards[1:]:
        loudness = loudness * one(*cut)
    return loudness


def setup_inputs(seed: int = 0) -> dict:
    key_list = jax.random.split(jax.random.key(seed), 3)
    return {
        "field": jnp.clip(jnp.exp(math.log(10.0) - 4.6051702 * jax.random.uniform(key_list[0], (NZ, NY, NX), jnp.float32) ** block_scale(key_list[0], (NZ, NY, NX), ((0, 4), (1, 16), (2, 4)), -0.2, 0.2)), 0.1, 10.0),
        "view_order": jax.random.permutation(key_list[1], N_DEPTH).astype(jnp.int32),
    }


def render(padded, opacity_scale):
    depth_cells = padded.shape[0] - 4
    row_cells = padded.shape[1] - 4
    col_cells = padded.shape[2] - 4

    def offset_view(shift_z, shift_y, shift_x):
        return padded[2 + shift_z:2 + shift_z + depth_cells, 2 + shift_y:2 + shift_y + row_cells, 2 + shift_x:2 + shift_x + col_cells]
    centre = offset_view(0, 0, 0)
    grad_z = (8.0 * (offset_view(1, 0, 0) - offset_view(-1, 0, 0)) - (offset_view(2, 0, 0) - offset_view(-2, 0, 0))) / 12.0
    grad_y = (8.0 * (offset_view(0, 1, 0) - offset_view(0, -1, 0)) - (offset_view(0, 2, 0) - offset_view(0, -2, 0))) / 12.0
    grad_x = (8.0 * (offset_view(0, 0, 1) - offset_view(0, 0, -1)) - (offset_view(0, 0, 2) - offset_view(0, 0, -2))) / 12.0
    shading = 0.3 + 0.7 * jnp.abs(0.48 * grad_z + 0.6 * grad_y + 0.64 * grad_x) / jnp.sqrt(grad_z * grad_z + grad_y * grad_y + grad_x * grad_x + 1.0)
    bright = centre / (1.0 + centre)
    tau = opacity_scale * 2.0 * bright
    inclusive = jnp.cumsum(tau, axis=0)
    weight = jnp.exp(-(inclusive - tau)) * (1.0 - jnp.exp(-tau)) * 2.0 * shading
    red_sum = lax.optimization_barrier(jnp.sum(weight * bright, axis=0))
    green_sum = lax.optimization_barrier(jnp.sum(weight / (1.0 + centre), axis=0))
    blue_sum = lax.optimization_barrier(jnp.sum(weight * 4.0 * bright / (1.0 + centre), axis=0))
    through = jnp.exp(-inclusive[-1])
    return (jnp.stack([red_sum, green_sum, blue_sum]), through)

def reference(field, view_order):
    opacity_scale = 1.5 / NZ

    def render_brick(brick):
        slab_rows = ((brick * CZ - 2 + jnp.arange(CZ + 4)) % NZ).astype(jnp.int32)
        slab_cells = jnp.take(field, slab_rows, axis=0)
        padded = jnp.pad(slab_cells, ((0, 0), (2, 2), (2, 2)), mode='wrap')
        return render(padded, opacity_scale)
    colors, through = lax.map(render_brick, jnp.arange(N_DEPTH, dtype=jnp.int32))
    positions = jnp.arange(N_DEPTH, dtype=jnp.int32)
    view_rank = lax.optimization_barrier(jnp.sum(positions[None, :] * (view_order[None, :] == positions[:, None]).astype(jnp.int32), axis=1))
    in_front = view_rank[None, :] < view_rank[:, None]
    factor = jnp.prod(jnp.where(in_front[:, :, None, None], through[None], 1.0), axis=1)
    color_image = lax.optimization_barrier(jnp.sum(factor[:, None] * colors, axis=0))
    opacity = lax.optimization_barrier(jnp.sum(factor * (1.0 - through), axis=0))
    return jnp.concatenate([color_image, opacity[None]], axis=0)
```

```python
import math

import jax
import jax.numpy as jnp
from jax import lax
from jax.experimental import pallas as pl
from jax.experimental.pallas import tpu as pltpu
from jax.sharding import PartitionSpec as P

MESH = pl.DeviceIdType.MESH
CZ, NY, NX = 32, 128, 512
NB = 4
GROUPS = 4
STEP = 4
TILES = ((1, 2), (0, 3))
KEXP = -1.5 * 2.0 / 128.0
BIAS = 0.3 / 0.448
SCALE = 2.0 * 0.448


def kernel(vo_ref, f_ref, o_ref, buf, xs, xr, stage, recv, fin, fbuf,
           ld, zss, zrs, yss, yrs, xss, xrs, ass, ars, fss, frs):
    d, r, c = lax.axis_index("depth"), lax.axis_index("row"), lax.axis_index("col")
    brick = lambda k: (lax.rem(d + k, NB), r, c)
    row_to = (lax.rem(r + 1, 16), lax.rem(r + 15, 16))
    col_to = (lax.rem(c + 1, 4), lax.rem(c + 3, 4))
    lane = lax.broadcasted_iota(jnp.int32, (8, 128), 1)

    barrier = pltpu.get_barrier_semaphore()
    others = [brick(1), brick(2), brick(3), (d, row_to[0], c), (d, row_to[1], c),
              (d, r, col_to[0]), (d, r, col_to[1])]
    for dev in others:
        pl.semaphore_signal(barrier, inc=1, device_id=dev, device_id_type=MESH)

    def load(t, g):
        return pltpu.make_async_copy(
            f_ref.at[:, pl.ds(32 * g, 32), pl.ds(128 * t, 128)],
            buf.at[pl.ds(2, CZ), t, pl.ds(8 + 32 * g, 32), :], ld.at[t, g])

    def zhalo(p, i, side, n):
        t, g = TILES[p][n], lax.rem(i + 1, GROUPS)
        src, dst, k = ((CZ - 2, 0, 1), (0, CZ + 2, 3))[side]
        return pltpu.make_async_remote_copy(
            f_ref.at[pl.ds(src, 2), pl.ds(32 * g, 32), pl.ds(128 * t, 128)],
            buf.at[pl.ds(dst, 2), t, pl.ds(8 + 32 * g, 32), :],
            zss.at[p, i, side, n], zrs.at[p, i, side, n],
            device_id=brick(k), device_id_type=MESH)

    def yhalo(t, side):
        src, dst = ((NY - 8, 0), (0, NY + 8))[side]
        return pltpu.make_async_remote_copy(
            f_ref.at[:, pl.ds(src, 8), pl.ds(128 * t, 128)],
            buf.at[pl.ds(2, CZ), t, pl.ds(dst, 8), :],
            yss.at[t, side], yrs.at[t, side],
            device_id=(d, row_to[side], c), device_id_type=MESH)

    def xhalo(side):
        return pltpu.make_async_remote_copy(
            xs, xr.at[side], xss.at[side], xrs.at[side],
            device_id=(d, r, col_to[side]), device_id_type=MESH)

    def part(j, k):
        return pltpu.make_async_remote_copy(
            stage.at[j, lax.rem(d + k, NB)], recv.at[j, k - 1],
            ass.at[j, k - 1], ars.at[j, k - 1],
            device_id=brick(k), device_id_type=MESH)

    def final(j, k, owner):
        p, g = j // GROUPS, lax.rem(j + 1, GROUPS)
        return pltpu.make_async_remote_copy(
            fin.at[j, lax.rem(d + k, NB)],
            fbuf.at[pl.ds(2 * p, 2), pl.ds(32 * g + 8 * owner, 8), :],
            fss.at[j, k - 1], frs.at[j, k - 1],
            device_id=brick(k), device_id_type=MESH)

    for t in (0, 3, 1, 2):
        for g in range(GROUPS):
            load(t, g).start()
    pl.semaphore_wait(barrier, len(others))

    for p in range(2):
        @pl.loop(0, GROUPS)
        def _(i):
            for side in range(2):
                for n in range(2):
                    zhalo(p, i, side, n).start()
    for side in (1, 0):
        for t in (1, 2, 0, 3):
            yhalo(t, side).start()

    for t in (0, 3):
        for g in range(GROUPS):
            load(t, g).wait()

    @pl.loop(0, NY // 8)
    def _(t):
        rows = pl.ds(pl.multiple_of(8 + 8 * t, 8), 8)
        left = [buf[2 + z, 0, rows, :] for z in range(CZ)]
        right = [buf[2 + z, 3, rows, :] for z in range(CZ)]
        w = 2
        while len(left) > 1:
            left = [jnp.where(lane < w, a, pltpu.roll(b, w, 1)) for a, b in zip(left[::2], left[1::2])]
            right = [jnp.where(lane >= 128 - w, b, pltpu.roll(a, 128 - w, 1)) for a, b in zip(right[::2], right[1::2])]
            w *= 2
        xs[pl.ds(pl.multiple_of(8 * t, 8), 8), :] = jnp.where(lane < 64, left[0], right[0])

    for side in range(2):
        xhalo(side).start()
    for t in (1, 2):
        for g in range(GROUPS):
            load(t, g).wait()

    def strip(p, j, g, q):
        row = pl.multiple_of(8 + 32 * g + 8 * q, 8)
        rows = pl.ds(row, 8)
        tiles = TILES[p]
        edge_rows = pl.ds(pl.multiple_of(32 * g + 8 * q, 8), 8)
        if p == 1:
            from_left, from_right = xr[0, edge_rows, :], xr[1, edge_rows, :]

        def body(zz, carry):
            z0 = zz * STEP
            state = list(carry)
            col = {t: [buf[z0 + m, t, rows, :] for m in range(STEP + 4)] for t in tiles}
            for m in range(STEP):
                z = z0 + m
                for n, t in enumerate(tiles):
                    energy, wsum, rsum, bsum = state[4 * n:4 * n + 4]
                    s = col[t][m + 2]
                    gz = 8.0 * (col[t][m + 3] - col[t][m + 1]) - (col[t][m + 4] - col[t][m])
                    yv = lambda o: buf[z + 2, t, pl.ds(row + o, 8), :]
                    gy = 8.0 * (yv(1) - yv(-1)) - (yv(2) - yv(-2))
                    if t == 0:
                        prv = pltpu.roll(from_left, 62 - 2 * z, 1)
                    elif t - 1 in tiles:
                        prv = col[t - 1][m + 2]
                    else:
                        prv = buf[z + 2, t - 1, rows, :]
                    if t == 3:
                        nxt = pltpu.roll(from_right, lax.rem(128 - 2 * z, 128), 1)
                    elif t + 1 in tiles:
                        nxt = col[t + 1][m + 2]
                    else:
                        nxt = buf[z + 2, t + 1, rows, :]
                    xp1 = pltpu.roll(jnp.where(lane < 1, nxt, s), 127, 1)
                    xp2 = pltpu.roll(jnp.where(lane < 2, nxt, s), 126, 1)
                    xm1 = pltpu.roll(jnp.where(lane >= 127, prv, s), 1, 1)
                    xm2 = pltpu.roll(jnp.where(lane >= 126, prv, s), 2, 1)
                    gx = 8.0 * (xp1 - xm1) - (xp2 - xm2)
                    norm = (gz * gz + gy * gy) + (gx * gx + 144.0)
                    along = (0.75 * gz + 0.9375 * gy) + gx
                    shade = jnp.abs(along) * lax.rsqrt(norm) + BIAS
                    recip = pl.reciprocal(1.0 + s)
                    bright = 1.0 - recip
                    after = energy * jnp.exp(bright * KEXP)
                    weight = (energy - after) * shade
                    red = weight * bright
                    state[4 * n:4 * n + 4] = [after, wsum + weight, rsum + red, bsum + red * recip]
            return tuple(state)

        one, zero = jnp.ones((8, 128), jnp.float32), jnp.zeros((8, 128), jnp.float32)
        state = lax.fori_loop(0, CZ // STEP, body, (one, zero, zero, zero) * 2)
        for n in range(2):
            energy, wsum, rsum, bsum = state[4 * n:4 * n + 4]
            stage[j, q, 0 + n] = SCALE * rsum
            stage[j, q, 2 + n] = SCALE * (wsum - rsum)
            stage[j, q, 4 + n] = 4.0 * SCALE * bsum
            stage[j, q, 6 + n] = energy

    for p in range(2):
        if p == 1:
            for side in range(2):
                xhalo(side).wait()

        @pl.loop(0, GROUPS)
        def _(i):
            j, g = GROUPS * p + i, lax.rem(i + 1, GROUPS)
            for side in range(2):
                for n in range(2):
                    zhalo(p, i, side, n).wait()
            if p == 0:
                for side, at in ((1, 2), (0, 3)):
                    @pl.when(i == at)
                    def _():
                        for t in range(4):
                            yhalo(t, side).wait()

            @pl.loop(0, 4)
            def _(q):
                strip(p, j, g, q)

            for k in range(1, NB):
                part(j, k).start()

    ranks = []
    for k in range(NB):
        b = lax.rem(d + NB - k, NB)
        rank = jnp.int32(0)
        for pos in range(1, NB):
            rank = rank + jnp.where(vo_ref[pos] == b, jnp.int32(pos), jnp.int32(0))
        ranks.append(jnp.full((8, 128), rank, jnp.int32))
    ahead = [[None if e == k else ranks[e] < ranks[k] for e in range(NB)] for k in range(NB)]

    for p in range(2):
        @pl.loop(0, GROUPS)
        def _(i):
            j, g = GROUPS * p + i, lax.rem(i + 1, GROUPS)
            for k in range(1, NB):
                part(j, k).wait()
            for n in range(2):
                get = lambda k, ch: stage[j, d, 2 * ch + n] if k == 0 else recv[j, k - 1, 2 * ch + n]
                through = [get(k, 3) for k in range(NB)]
                total = [jnp.zeros((8, 128), jnp.float32)] * 4
                for k in range(NB):
                    factor = jnp.ones((8, 128), jnp.float32)
                    for e in range(NB):
                        if e != k:
                            factor = factor * jnp.where(ahead[k][e], through[e], 1.0)
                    for ch in range(3):
                        total[ch] = total[ch] + factor * get(k, ch)
                    total[3] = total[3] + factor * (1.0 - through[k])
                for ch in range(4):
                    fin[j, ch, n] = total[ch]
            for k in range(1, NB):
                final(j, k, d).start()
            fbuf[pl.ds(2 * p, 2), pl.ds(pl.multiple_of(32 * g + 8 * d, 8), 8), :] = fin[j, d]

    @pl.loop(0, 2 * GROUPS)
    def _(j):
        for k in range(1, NB):
            final(j, k, lax.rem(d + NB - k, NB)).wait()

    for p in range(2):
        for n in range(2):
            o_ref[0, :, pl.ds(128 * TILES[p][n], 128)] = fbuf[2 * p + n]


def per_device(field, view_order):
    dma = pltpu.SemaphoreType.DMA
    vmem = lambda *shape: pltpu.VMEM(shape, jnp.float32)
    return pl.pallas_call(
        kernel,
        out_shape=jax.ShapeDtypeStruct((1, NY, NX), jnp.float32),
        in_specs=[pl.BlockSpec(memory_space=pltpu.SMEM), pl.BlockSpec(memory_space=pl.ANY)],
        out_specs=pl.BlockSpec(memory_space=pltpu.VMEM),
        scratch_shapes=[
            vmem(CZ + 4, 4, NY + 16, 128),
            vmem(NY, 128), vmem(2, NY, 128),
            vmem(8, 4, 8, 8, 128), vmem(8, 3, 8, 8, 128),
            vmem(8, 4, 2, 8, 128), vmem(4, NY, 128),
            dma((4, 4)), dma((2, 4, 2, 2)), dma((2, 4, 2, 2)), dma((4, 2)), dma((4, 2)),
            dma((2,)), dma((2,)), dma((8, 3)), dma((8, 3)), dma((8, 3)), dma((8, 3)),
        ],
        compiler_params=pltpu.CompilerParams(
            collective_id=0, has_side_effects=True, vmem_limit_bytes=48 << 20),
    )(view_order, field)


def solution(mesh):
    return jax.shard_map(
        per_device, mesh=mesh, in_specs=(P("depth", "row", "col"), P()),
        out_specs=P("depth", "row", "col"), check_vma=False)
```

```python
import math

import jax
import jax.numpy as jnp
from jax import lax
from jax.experimental import pallas as pl
from jax.experimental.pallas import tpu as pltpu
from jax.sharding import PartitionSpec as P

MESH = pl.DeviceIdType.MESH
CZ, NY, NX = 32, 128, 512
NB = 4
GROUPS = 4
STEP = 16
TILES = ((1, 2), (0, 3))
KEXP = -1.5 * 2.0 / 128.0 * math.log2(math.e)
BIAS = 0.3 / 0.448
SCALE = 2.0 * 0.448


def kernel(vo_ref, f_ref, o_ref, buf, xs, xr, stage, recv, fin, fbuf,
           ld, zss, zrs, yss, yrs, xss, xrs, ass, ars, fss, frs):
    d, r, c = lax.axis_index("depth"), lax.axis_index("row"), lax.axis_index("col")
    brick = lambda k: (lax.rem(d + k, NB), r, c)
    row_to = (lax.rem(r + 1, 16), lax.rem(r + 15, 16))
    col_to = (lax.rem(c + 1, 4), lax.rem(c + 3, 4))
    lane = lax.broadcasted_iota(jnp.int32, (8, 128), 1)
    pair = lane // 2

    barrier = pltpu.get_barrier_semaphore()
    others = [brick(1), brick(2), brick(3), (d, row_to[0], c), (d, row_to[1], c),
              (d, r, col_to[0]), (d, r, col_to[1])]
    for dev in others:
        pl.semaphore_signal(barrier, inc=1, device_id=dev, device_id_type=MESH)

    def load(t, g):
        return pltpu.make_async_copy(
            f_ref.at[:, pl.ds(32 * g, 32), pl.ds(128 * t, 128)],
            buf.at[pl.ds(2, CZ), t, pl.ds(8 + 32 * g, 32), :], ld.at[t, g])

    def zhalo(p, i, side, n):
        t, g = TILES[p][n], lax.rem(i + 1, GROUPS)
        src, dst, k = ((CZ - 2, 0, 1), (0, CZ + 2, 3))[side]
        return pltpu.make_async_remote_copy(
            f_ref.at[pl.ds(src, 2), pl.ds(32 * g, 32), pl.ds(128 * t, 128)],
            buf.at[pl.ds(dst, 2), t, pl.ds(8 + 32 * g, 32), :],
            zss.at[p, i, side, n], zrs.at[p, i, side, n],
            device_id=brick(k), device_id_type=MESH)

    def yhalo(t, side):
        src, dst = ((NY - 8, 0), (0, NY + 8))[side]
        return pltpu.make_async_remote_copy(
            f_ref.at[:, pl.ds(src, 8), pl.ds(128 * t, 128)],
            buf.at[pl.ds(2, CZ), t, pl.ds(dst, 8), :],
            yss.at[t, side], yrs.at[t, side],
            device_id=(d, row_to[side], c), device_id_type=MESH)

    def xhalo(side):
        return pltpu.make_async_remote_copy(
            xs, xr.at[side], xss.at[side], xrs.at[side],
            device_id=(d, r, col_to[side]), device_id_type=MESH)

    def part(j, k):
        return pltpu.make_async_remote_copy(
            stage.at[j, lax.rem(d + k, NB)], recv.at[j, k - 1],
            ass.at[j, k - 1], ars.at[j, k - 1],
            device_id=brick(k), device_id_type=MESH)

    def final(j, k, owner):
        p, g = j // GROUPS, lax.rem(j + 1, GROUPS)
        return pltpu.make_async_remote_copy(
            fin.at[j, lax.rem(d + k, NB)],
            fbuf.at[pl.ds(2 * p, 2), pl.ds(32 * g + 8 * owner, 8), :],
            fss.at[j, k - 1], frs.at[j, k - 1],
            device_id=brick(k), device_id_type=MESH)

    for t in (0, 3, 1, 2):
        for g in range(GROUPS):
            load(t, g).start()
    pl.semaphore_wait(barrier, len(others))

    for p in range(2):
        @pl.loop(0, GROUPS)
        def _(i):
            for side in range(2):
                for n in range(2):
                    zhalo(p, i, side, n).start()
    for side in (1, 0):
        for t in (1, 2, 0, 3):
            yhalo(t, side).start()

    for t in (0, 3):
        for g in range(GROUPS):
            load(t, g).wait()

    @pl.loop(0, NY // 8, unroll=2)
    def _(t):
        rows = pl.ds(pl.multiple_of(8 + 8 * t, 8), 8)
        faces = jnp.zeros((8, 128), jnp.float32)
        for z in range(CZ):
            left = pltpu.roll(buf[2 + z, 0, rows, :], 2 * z, 1) if z else buf[2, 0, rows, :]
            right = pltpu.roll(buf[2 + z, 3, rows, :], 66 + 2 * z, 1)
            faces = jnp.where(pair == z, left, jnp.where(pair == 32 + z, right, faces))
        xs[pl.ds(pl.multiple_of(8 * t, 8), 8), :] = faces

    for side in range(2):
        xhalo(side).start()
    for t in (1, 2):
        for g in range(GROUPS):
            load(t, g).wait()

    def strip(p, j, g, q):
        row = pl.multiple_of(8 + 32 * g + 8 * q, 8)
        rows = pl.ds(row, 8)
        tiles = TILES[p]
        edge_rows = pl.ds(pl.multiple_of(32 * g + 8 * q, 8), 8)
        if p == 1:
            from_left, from_right = xr[0, edge_rows, :], xr[1, edge_rows, :]

        def body(zz, carry):
            z0 = zz * STEP
            state = list(carry)
            col = {t: [buf[z0 + m, t, rows, :] for m in range(STEP + 4)] for t in tiles}
            for m in range(STEP):
                z = z0 + m
                for n, t in enumerate(tiles):
                    energy, wsum, rsum, bsum = state[4 * n:4 * n + 4]
                    s = col[t][m + 2]
                    gz = 8.0 * (col[t][m + 3] - col[t][m + 1]) - (col[t][m + 4] - col[t][m])
                    yv = lambda o: buf[z + 2, t, pl.ds(row + o, 8), :]
                    gy = 8.0 * (yv(1) - yv(-1)) - (yv(2) - yv(-2))
                    if t == 0:
                        prv = pltpu.roll(from_left, 62 - 2 * z, 1)
                    elif t - 1 in tiles:
                        prv = col[t - 1][m + 2]
                    else:
                        prv = buf[z + 2, t - 1, rows, :]
                    if t == 3:
                        nxt = pltpu.roll(from_right, lax.rem(128 - 2 * z, 128), 1)
                    elif t + 1 in tiles:
                        nxt = col[t + 1][m + 2]
                    else:
                        nxt = buf[z + 2, t + 1, rows, :]
                    xp1 = pltpu.roll(jnp.where(lane < 1, nxt, s), 127, 1)
                    xp2 = pltpu.roll(jnp.where(lane < 2, nxt, s), 126, 1)
                    xm1 = pltpu.roll(jnp.where(lane >= 127, prv, s), 1, 1)
                    xm2 = pltpu.roll(jnp.where(lane >= 126, prv, s), 2, 1)
                    gx = 8.0 * (xp1 - xm1) - (xp2 - xm2)
                    norm = (gz * gz + gy * gy) + (gx * gx + 144.0)
                    along = (0.75 * gz + 0.9375 * gy) + gx
                    shade = jnp.abs(along) * lax.rsqrt(norm) + BIAS
                    recip = pl.reciprocal(1.0 + s)
                    bright = 1.0 - recip
                    after = energy * jnp.exp2(bright * KEXP)
                    weight = (energy - after) * shade
                    red = weight * bright
                    state[4 * n:4 * n + 4] = [after, wsum + weight, rsum + red, bsum + red * recip]
            return tuple(state)

        one, zero = jnp.ones((8, 128), jnp.float32), jnp.zeros((8, 128), jnp.float32)
        state = lax.fori_loop(0, CZ // STEP, body, (one, zero, zero, zero) * 2)
        for n in range(2):
            energy, wsum, rsum, bsum = state[4 * n:4 * n + 4]
            stage[j, q, 0 + n] = SCALE * rsum
            stage[j, q, 2 + n] = SCALE * (wsum - rsum)
            stage[j, q, 4 + n] = 4.0 * SCALE * bsum
            stage[j, q, 6 + n] = energy

    for p in range(2):
        if p == 1:
            for side in range(2):
                xhalo(side).wait()

        @pl.loop(0, GROUPS)
        def _(i):
            j, g = GROUPS * p + i, lax.rem(i + 1, GROUPS)
            for side in range(2):
                for n in range(2):
                    zhalo(p, i, side, n).wait()
            if p == 0:
                for side, at in ((1, 2), (0, 3)):
                    @pl.when(i == at)
                    def _():
                        for t in range(4):
                            yhalo(t, side).wait()

            @pl.loop(0, 4)
            def _(q):
                strip(p, j, g, q)

            for k in range(1, NB):
                part(j, k).start()

    ranks = []
    for k in range(NB):
        b = lax.rem(d + NB - k, NB)
        rank = jnp.int32(0)
        for pos in range(1, NB):
            rank = rank + jnp.where(vo_ref[pos] == b, jnp.int32(pos), jnp.int32(0))
        ranks.append(jnp.full((8, 128), rank, jnp.int32))
    ahead = [[None if e == k else ranks[e] < ranks[k] for e in range(NB)] for k in range(NB)]

    for p in range(2):
        @pl.loop(0, GROUPS)
        def _(i):
            j, g = GROUPS * p + i, lax.rem(i + 1, GROUPS)
            for k in range(1, NB):
                part(j, k).wait()
            for n in range(2):
                get = lambda k, ch: stage[j, d, 2 * ch + n] if k == 0 else recv[j, k - 1, 2 * ch + n]
                through = [get(k, 3) for k in range(NB)]
                total = [jnp.zeros((8, 128), jnp.float32)] * 4
                for k in range(NB):
                    factor = jnp.ones((8, 128), jnp.float32)
                    for e in range(NB):
                        if e != k:
                            factor = factor * jnp.where(ahead[k][e], through[e], 1.0)
                    for ch in range(3):
                        total[ch] = total[ch] + factor * get(k, ch)
                    total[3] = total[3] + factor * (1.0 - through[k])
                for ch in range(4):
                    fin[j, ch, n] = total[ch]
            for k in range(1, NB):
                final(j, k, d).start()
            fbuf[pl.ds(2 * p, 2), pl.ds(pl.multiple_of(32 * g + 8 * d, 8), 8), :] = fin[j, d]

    @pl.loop(0, 2 * GROUPS)
    def _(j):
        for k in range(1, NB):
            final(j, k, lax.rem(d + NB - k, NB)).wait()

    for p in range(2):
        for n in range(2):
            o_ref[0, :, pl.ds(128 * TILES[p][n], 128)] = fbuf[2 * p + n]


def per_device(field, view_order):
    dma = pltpu.SemaphoreType.DMA
    vmem = lambda *shape: pltpu.VMEM(shape, jnp.float32)
    return pl.pallas_call(
        kernel,
        out_shape=jax.ShapeDtypeStruct((1, NY, NX), jnp.float32),
        in_specs=[pl.BlockSpec(memory_space=pltpu.SMEM), pl.BlockSpec(memory_space=pl.ANY)],
        out_specs=pl.BlockSpec(memory_space=pltpu.VMEM),
        scratch_shapes=[
            vmem(CZ + 4, 4, NY + 16, 128),
            vmem(NY, 128), vmem(2, NY, 128),
            vmem(8, 4, 8, 8, 128), vmem(8, 3, 8, 8, 128),
            vmem(8, 4, 2, 8, 128), vmem(4, NY, 128),
            dma((4, 4)), dma((2, 4, 2, 2)), dma((2, 4, 2, 2)), dma((4, 2)), dma((4, 2)),
            dma((2,)), dma((2,)), dma((8, 3)), dma((8, 3)), dma((8, 3)), dma((8, 3)),
        ],
        compiler_params=pltpu.CompilerParams(
            collective_id=0, has_side_effects=True, vmem_limit_bytes=48 << 20),
    )(view_order, field)


def solution(mesh):
    return jax.shard_map(
        per_device, mesh=mesh, in_specs=(P("depth", "row", "col"), P()),
        out_specs=P("depth", "row", "col"), check_vma=False)
```

```python
import math

import jax
import jax.numpy as jnp
from jax import lax
from jax.experimental import pallas as pl
from jax.experimental.pallas import tpu as pltpu
from jax.sharding import PartitionSpec as P

MESH = pl.DeviceIdType.MESH
CZ, NY, NX = 32, 128, 512
NB = 4
GROUPS = 4
STEP = 32
TILES = ((1, 2), (0, 3))
KEXP = -1.5 * 2.0 / 128.0 * math.log2(math.e)
BIAS = 0.3 / 0.448
SCALE = 2.0 * 0.448


def kernel(vo_ref, f_ref, o_ref, buf, xs, xr, stage, recv, fin, fbuf,
           ld, zss, zrs, yss, yrs, xss, xrs, ass, ars, fss, frs):
    d, r, c = lax.axis_index("depth"), lax.axis_index("row"), lax.axis_index("col")
    brick = lambda k: (lax.rem(d + k, NB), r, c)
    row_to = (lax.rem(r + 1, 16), lax.rem(r + 15, 16))
    col_to = (lax.rem(c + 1, 4), lax.rem(c + 3, 4))
    lane = lax.broadcasted_iota(jnp.int32, (8, 128), 1)

    barrier = pltpu.get_barrier_semaphore()
    others = [brick(1), brick(2), brick(3), (d, row_to[0], c), (d, row_to[1], c),
              (d, r, col_to[0]), (d, r, col_to[1])]
    for dev in others:
        pl.semaphore_signal(barrier, inc=1, device_id=dev, device_id_type=MESH)

    def load(t, g):
        return pltpu.make_async_copy(
            f_ref.at[:, pl.ds(32 * g, 32), pl.ds(128 * t, 128)],
            buf.at[pl.ds(2, CZ), t, pl.ds(8 + 32 * g, 32), :], ld.at[t, g])

    def zhalo(p, i, side, n):
        t, g = jnp.where(p == 0, n + 1, 3 * n), lax.rem(i + 1, GROUPS)
        src, dst, k = ((CZ - 2, 0, 1), (0, CZ + 2, 3))[side]
        return pltpu.make_async_remote_copy(
            f_ref.at[pl.ds(src, 2), pl.ds(32 * g, 32), pl.ds(128 * t, 128)],
            buf.at[pl.ds(dst, 2), t, pl.ds(8 + 32 * g, 32), :],
            zss.at[p, i, side, n], zrs.at[p, i, side, n],
            device_id=brick(k), device_id_type=MESH)

    def yhalo(t, side):
        src, dst = ((NY - 8, 0), (0, NY + 8))[side]
        return pltpu.make_async_remote_copy(
            f_ref.at[:, pl.ds(src, 8), pl.ds(128 * t, 128)],
            buf.at[pl.ds(2, CZ), t, pl.ds(dst, 8), :],
            yss.at[t, side], yrs.at[t, side],
            device_id=(d, row_to[side], c), device_id_type=MESH)

    def xhalo(side):
        return pltpu.make_async_remote_copy(
            xs, xr.at[side], xss.at[side], xrs.at[side],
            device_id=(d, r, col_to[side]), device_id_type=MESH)

    def part(j, k):
        return pltpu.make_async_remote_copy(
            stage.at[j, lax.rem(d + k, NB)], recv.at[j, k - 1],
            ass.at[j, k - 1], ars.at[j, k - 1],
            device_id=brick(k), device_id_type=MESH)

    def final(j, k, owner):
        p, g = j // GROUPS, lax.rem(j + 1, GROUPS)
        return pltpu.make_async_remote_copy(
            fin.at[j, lax.rem(d + k, NB)],
            fbuf.at[pl.ds(2 * p, 2), pl.ds(32 * g + 8 * owner, 8), :],
            fss.at[j, k - 1], frs.at[j, k - 1],
            device_id=brick(k), device_id_type=MESH)

    for t in (0, 3, 1, 2):
        for g in range(GROUPS):
            load(t, g).start()

    pl.semaphore_wait(barrier, len(others))

    @pl.loop(0, 2 * GROUPS)
    def _(j):
        for side in range(2):
            for n in range(2):
                zhalo(j // GROUPS, lax.rem(j, GROUPS), side, n).start()

    for side in (1, 0):
        for t in (1, 2, 0, 3):
            yhalo(t, side).start()

    for t in (0, 3):
        for g in range(GROUPS):
            load(t, g).wait()

    @pl.loop(0, NY // 8, unroll=2)
    def _(t):
        rows = pl.ds(pl.multiple_of(8 + 8 * t, 8), 8)
        faces = jnp.zeros((8, 128), jnp.float32)
        for z in range(CZ):
            ends = jnp.where(lane < 64, buf[2 + z, 0, rows, :], buf[2 + z, 3, rows, :])
            ends = pltpu.roll(ends, 4 * z, 1) if z else ends
            faces = jnp.where(lax.rem(lane + 2, 128) // 4 == z, ends, faces)
        xs[pl.ds(pl.multiple_of(8 * t, 8), 8), :] = faces

    for side in range(2):
        xhalo(side).start()
    for t in (1, 2):
        for g in range(GROUPS):
            load(t, g).wait()

    def tile_of(j, n):
        return jnp.where(j < GROUPS, n + 1, 3 * n)

    def strip(j, q):
        g = lax.rem(j + 1, GROUPS)
        row = pl.multiple_of(8 + 32 * g + 8 * q, 8)
        rows = pl.ds(row, 8)
        tiles = tile_of(j, 0), tile_of(j, 1)

        def body(zz, carry):
            z0 = zz * STEP
            state = list(carry)
            for n, t in enumerate(tiles):
                col = [buf[z0 + m, t, rows, :] for m in range(STEP + 4)]
                for m in range(STEP):
                    z = z0 + m
                    energy, wsum, rsum, bsum = state[4 * n:4 * n + 4]
                    s = col[m + 2]
                    gz = 8.0 * (col[m + 3] - col[m + 1]) - (col[m + 4] - col[m])
                    yv = lambda o: buf[z + 2, t, pl.ds(row + o, 8), :]
                    gy = 8.0 * (yv(1) - yv(-1)) - (yv(2) - yv(-2))
                    prv, nxt = buf[z + 2, lax.rem(t + 4, 5), rows, :], buf[z + 2, t + 1, rows, :]
                    xp1 = pltpu.roll(jnp.where(lane < 1, nxt, s), 127, 1)
                    xp2 = pltpu.roll(jnp.where(lane < 2, nxt, s), 126, 1)
                    xm1 = pltpu.roll(jnp.where(lane >= 127, prv, s), 1, 1)
                    xm2 = pltpu.roll(jnp.where(lane >= 126, prv, s), 2, 1)
                    gx = 8.0 * (xp1 - xm1) - (xp2 - xm2)
                    norm = (gz * gz + gy * gy) + (gx * gx + 144.0)
                    along = (0.75 * gz + 0.9375 * gy) + gx
                    shade = jnp.abs(along) * lax.rsqrt(norm) + BIAS
                    recip = pl.reciprocal(1.0 + s)
                    bright = 1.0 - recip
                    after = energy * jnp.exp2(bright * KEXP)
                    weight = (energy - after) * shade
                    red = weight * bright
                    state[4 * n:4 * n + 4] = [after, wsum + weight, rsum + red, bsum + red * recip]
            return tuple(state)

        one, zero = jnp.ones((8, 128), jnp.float32), jnp.zeros((8, 128), jnp.float32)
        state = lax.fori_loop(0, CZ // STEP, body, (one, zero, zero, zero) * 2)
        for n in range(2):
            energy, wsum, rsum, bsum = state[4 * n:4 * n + 4]
            stage[j, q, 0 + n] = SCALE * rsum
            stage[j, q, 2 + n] = SCALE * (wsum - rsum)
            stage[j, q, 4 + n] = 4.0 * SCALE * bsum
            stage[j, q, 6 + n] = energy

    @pl.loop(0, 2 * GROUPS)
    def _(j):
        for side in range(2):
            for n in range(2):
                zhalo(j // GROUPS, lax.rem(j, GROUPS), side, n).wait()
        for side, at in ((1, 2), (0, 3)):
            @pl.when(j == at)
            def _():
                for t in range(4):
                    yhalo(t, side).wait()

        @pl.when(j == 2)
        def _():
            for side in range(2):
                xhalo(side).wait()

            @pl.loop(0, NY // 8)
            def _(t):
                rows = pl.ds(pl.multiple_of(8 * t, 8), 8)
                beyond = jnp.where(lax.rem(lane, 4) >= 2, xr[0, rows, :], xr[1, rows, :])
                for z in range(CZ):
                    buf[z + 2, 4, pl.ds(pl.multiple_of(8 * t + 8, 8), 8), :] = pltpu.roll(beyond, 128 - 4 * z, 1) if z else beyond

        @pl.loop(0, 4)
        def _(q):
            strip(j, q)

        for k in range(1, NB):
            part(j, k).start()

    ranks = []
    for k in range(NB):
        b = lax.rem(d + NB - k, NB)
        rank = jnp.int32(0)
        for pos in range(1, NB):
            rank = rank + jnp.where(vo_ref[pos] == b, jnp.int32(pos), jnp.int32(0))
        ranks.append(jnp.full((8, 128), rank, jnp.int32))
    ahead = [[None if e == k else ranks[e] < ranks[k] for e in range(NB)] for k in range(NB)]

    for p in range(2):
        @pl.loop(0, GROUPS)
        def _(i):
            j, g = GROUPS * p + i, lax.rem(i + 1, GROUPS)
            for k in range(1, NB):
                part(j, k).wait()
            for n in range(2):
                get = lambda k, ch: stage[j, d, 2 * ch + n] if k == 0 else recv[j, k - 1, 2 * ch + n]
                through = [get(k, 3) for k in range(NB)]
                total = [jnp.zeros((8, 128), jnp.float32)] * 4
                for k in range(NB):
                    factor = jnp.ones((8, 128), jnp.float32)
                    for e in range(NB):
                        if e != k:
                            factor = factor * jnp.where(ahead[k][e], through[e], 1.0)
                    for ch in range(3):
                        total[ch] = total[ch] + factor * get(k, ch)
                    total[3] = total[3] + factor * (1.0 - through[k])
                for ch in range(4):
                    fin[j, ch, n] = total[ch]
            for k in range(1, NB):
                final(j, k, d).start()
            fbuf[pl.ds(2 * p, 2), pl.ds(pl.multiple_of(32 * g + 8 * d, 8), 8), :] = fin[j, d]

    @pl.loop(0, 2 * GROUPS)
    def _(j):
        for k in range(1, NB):
            final(j, k, lax.rem(d + NB - k, NB)).wait()

    for p in range(2):
        for n in range(2):
            o_ref[0, :, pl.ds(128 * TILES[p][n], 128)] = fbuf[2 * p + n]


def per_device(field, view_order):
    dma = pltpu.SemaphoreType.DMA
    vmem = lambda *shape: pltpu.VMEM(shape, jnp.float32)
    return pl.pallas_call(
        kernel,
        out_shape=jax.ShapeDtypeStruct((1, NY, NX), jnp.float32),
        in_specs=[pl.BlockSpec(memory_space=pltpu.SMEM), pl.BlockSpec(memory_space=pl.ANY)],
        out_specs=pl.BlockSpec(memory_space=pltpu.VMEM),
        scratch_shapes=[
            vmem(CZ + 4, 5, NY + 16, 128),
            vmem(NY, 128), vmem(2, NY, 128),
            vmem(8, 4, 8, 8, 128), vmem(8, 3, 8, 8, 128),
            vmem(8, 4, 2, 8, 128), vmem(4, NY, 128),
            dma((4, 4)), dma((2, 4, 2, 2)), dma((2, 4, 2, 2)), dma((4, 2)), dma((4, 2)),
            dma((2,)), dma((2,)), dma((8, 3)), dma((8, 3)), dma((8, 3)), dma((8, 3)),
        ],
        compiler_params=pltpu.CompilerParams(
            collective_id=0, has_side_effects=True, vmem_limit_bytes=48 << 20),
    )(view_order, field)


def solution(mesh):
    return jax.shard_map(
        per_device, mesh=mesh, in_specs=(P("depth", "row", "col"), P()),
        out_specs=P("depth", "row", "col"), check_vma=False)
```

```python
import math

import jax
import jax.numpy as jnp
from jax import lax
from jax.experimental import pallas as pl
from jax.experimental.pallas import tpu as pltpu
from jax.sharding import PartitionSpec as P

MESH = pl.DeviceIdType.MESH
CZ, NY, NX = 32, 128, 512
NB = 4
GROUPS = 4
STEP = 32
TILES = ((1, 2), (0, 3))
KEXP = -1.5 * 2.0 / 128.0 * math.log2(math.e)
BIAS = 0.3 / 0.448
SCALE = 2.0 * 0.448


def kernel(order_ref, f_ref, o_ref, vo_ref, buf, xs, xr, stage, recv, fin, fbuf,
           vs, ld, zss, zrs, yss, yrs, xss, xrs, ass, ars, fss, frs):
    d, r, c = lax.axis_index("depth"), lax.axis_index("row"), lax.axis_index("col")
    brick = lambda k: (lax.rem(d + k, NB), r, c)
    row_to = (lax.rem(r + 1, 16), lax.rem(r + 15, 16))
    col_to = (lax.rem(c + 1, 4), lax.rem(c + 3, 4))
    lane = lax.broadcasted_iota(jnp.int32, (8, 128), 1)

    barrier = pltpu.get_barrier_semaphore()
    others = [brick(1), brick(2), brick(3), (d, row_to[0], c), (d, row_to[1], c),
              (d, r, col_to[0]), (d, r, col_to[1])]
    for dev in others:
        pl.semaphore_signal(barrier, inc=1, device_id=dev, device_id_type=MESH)

    def load(t, g):
        return pltpu.make_async_copy(
            f_ref.at[:, pl.ds(32 * g, 32), pl.ds(128 * t, 128)],
            buf.at[pl.ds(2, CZ), t, pl.ds(8 + 32 * g, 32), :], ld.at[t, g])

    def zhalo(p, i, side, n):
        t, g = jnp.where(p == 0, n + 1, 3 * n), lax.rem(i + 1, GROUPS)
        src, dst, k = ((CZ - 2, 0, 1), (0, CZ + 2, 3))[side]
        return pltpu.make_async_remote_copy(
            f_ref.at[pl.ds(src, 2), pl.ds(32 * g, 32), pl.ds(128 * t, 128)],
            buf.at[pl.ds(dst, 2), t, pl.ds(8 + 32 * g, 32), :],
            zss.at[p, i, side, n], zrs.at[p, i, side, n],
            device_id=brick(k), device_id_type=MESH)

    def yhalo(t, side):
        src, dst = ((NY - 8, 0), (0, NY + 8))[side]
        return pltpu.make_async_remote_copy(
            f_ref.at[:, pl.ds(src, 8), pl.ds(128 * t, 128)],
            buf.at[pl.ds(2, CZ), t, pl.ds(dst, 8), :],
            yss.at[t, side], yrs.at[t, side],
            device_id=(d, row_to[side], c), device_id_type=MESH)

    def xhalo(side):
        return pltpu.make_async_remote_copy(
            xs, xr.at[side], xss.at[side], xrs.at[side],
            device_id=(d, r, col_to[side]), device_id_type=MESH)

    def part(j, k):
        return pltpu.make_async_remote_copy(
            stage.at[j, lax.rem(d + k, NB)], recv.at[j, k - 1],
            ass.at[j, k - 1], ars.at[j, k - 1],
            device_id=brick(k), device_id_type=MESH)

    def final(j, k, owner):
        p, g = j // GROUPS, lax.rem(j + 1, GROUPS)
        return pltpu.make_async_remote_copy(
            fin.at[j, lax.rem(d + k, NB)],
            fbuf.at[pl.ds(2 * p, 2), pl.ds(32 * g + 8 * owner, 8), :],
            fss.at[j, k - 1], frs.at[j, k - 1],
            device_id=brick(k), device_id_type=MESH)

    for t in (0, 3, 1, 2):
        for g in range(GROUPS):
            load(t, g).start(priority=1)

    order = pltpu.make_async_copy(order_ref, vo_ref, vs)
    order.start()
    pl.semaphore_wait(barrier, len(others))

    def send_zhalo(j):
        for n in range(2):
            for side in range(2):
                zhalo(j // GROUPS, lax.rem(j, GROUPS), side, n).start()

    pl.loop(0, 2 * GROUPS)(send_zhalo)

    for t in (0, 3):
        for g in range(GROUPS):
            load(t, g).wait()

    @pl.loop(0, NY // 8, unroll=2)
    def _(t):
        rows = pl.ds(pl.multiple_of(8 + 8 * t, 8), 8)
        faces = jnp.zeros((8, 128), jnp.float32)
        for z in range(CZ):
            ends = jnp.where(lane < 64, buf[2 + z, 0, rows, :], buf[2 + z, 3, rows, :])
            ends = pltpu.roll(ends, 4 * z, 1) if z else ends
            faces = jnp.where(lax.rem(lane + 2, 128) // 4 == z, ends, faces)
        xs[pl.ds(pl.multiple_of(8 * t, 8), 8), :] = faces

    for side in range(2):
        xhalo(side).start()
    for side in (1, 0):
        for t in (1, 2, 0, 3):
            yhalo(t, side).start()
    for t in (1, 2):
        for g in range(GROUPS):
            load(t, g).wait()

    def tile_of(j, n):
        return jnp.where(j < GROUPS, n + 1, 3 * n)

    def strip(j, q):
        g = lax.rem(j + 1, GROUPS)
        row = pl.multiple_of(8 + 32 * g + 8 * q, 8)
        rows = pl.ds(row, 8)
        tiles = tile_of(j, 0), tile_of(j, 1)

        def body(zz, carry):
            z0 = zz * STEP
            state = list(carry)
            for n, t in enumerate(tiles):
                col = [buf[z0 + m, t, rows, :] for m in range(STEP + 4)]
                for m in range(STEP):
                    z = z0 + m
                    energy, wsum, rsum, bsum = state[4 * n:4 * n + 4]
                    s = col[m + 2]
                    gz = 8.0 * (col[m + 3] - col[m + 1]) - (col[m + 4] - col[m])
                    yv = lambda o: buf[z + 2, t, pl.ds(row + o, 8), :]
                    gy = 8.0 * (yv(1) - yv(-1)) - (yv(2) - yv(-2))
                    prv, nxt = buf[z + 2, lax.rem(t + 4, 5), rows, :], buf[z + 2, t + 1, rows, :]
                    xp1 = pltpu.roll(jnp.where(lane < 1, nxt, s), 127, 1)
                    xp2 = pltpu.roll(jnp.where(lane < 2, nxt, s), 126, 1)
                    xm1 = pltpu.roll(jnp.where(lane >= 127, prv, s), 1, 1)
                    xm2 = pltpu.roll(jnp.where(lane >= 126, prv, s), 2, 1)
                    gx = 8.0 * (xp1 - xm1) - (xp2 - xm2)
                    norm = (gz * gz + gy * gy) + (gx * gx + 144.0)
                    along = (0.75 * gz + 0.9375 * gy) + gx
                    shade = jnp.abs(along) * lax.rsqrt(norm) + BIAS
                    recip = pl.reciprocal(1.0 + s)
                    bright = 1.0 - recip
                    after = energy * jnp.exp2(bright * KEXP)
                    weight = (energy - after) * shade
                    red = weight * bright
                    state[4 * n:4 * n + 4] = [after, wsum + weight, rsum + red, bsum + red * recip]
            return tuple(state)

        one, zero = jnp.ones((8, 128), jnp.float32), jnp.zeros((8, 128), jnp.float32)
        state = lax.fori_loop(0, CZ // STEP, body, (one, zero, zero, zero) * 2)
        for n in range(2):
            energy, wsum, rsum, bsum = state[4 * n:4 * n + 4]
            stage[j, q, 0 + n] = SCALE * rsum
            stage[j, q, 2 + n] = SCALE * (wsum - rsum)
            stage[j, q, 4 + n] = 4.0 * SCALE * bsum
            stage[j, q, 6 + n] = energy

    order.wait()
    ranks = []
    for k in range(NB):
        b = lax.rem(d + NB - k, NB)
        rank = jnp.int32(0)
        for pos in range(1, NB):
            rank = rank + jnp.where(vo_ref[pos] == b, jnp.int32(pos), jnp.int32(0))
        ranks.append(jnp.full((8, 128), rank, jnp.int32))
    ahead = [[None if e == k else ranks[e] < ranks[k] for e in range(NB)] for k in range(NB)]

    def blend(j):
        g = lax.rem(j + 1, GROUPS)
        for k in range(1, NB):
            part(j, k).wait_recv()
        for n in range(2):
            get = lambda k, ch: stage[j, d, 2 * ch + n] if k == 0 else recv[j, k - 1, 2 * ch + n]
            through = [get(k, 3) for k in range(NB)]
            total = [jnp.zeros((8, 128), jnp.float32)] * 4
            for k in range(NB):
                factor = jnp.ones((8, 128), jnp.float32)
                for e in range(NB):
                    if e != k:
                        factor = factor * jnp.where(ahead[k][e], through[e], 1.0)
                for ch in range(3):
                    total[ch] = total[ch] + factor * get(k, ch)
                total[3] = total[3] + factor * (1.0 - through[k])
            for ch in range(4):
                fin[j, ch, n] = total[ch]
        for k in range(1, NB):
            final(j, k, d).start()
        fbuf[pl.ds(2 * (j // GROUPS), 2), pl.ds(pl.multiple_of(32 * g + 8 * d, 8), 8), :] = fin[j, d]

    @pl.loop(0, 2 * GROUPS)
    def _(j):
        for side in range(2):
            for n in range(2):
                zhalo(j // GROUPS, lax.rem(j, GROUPS), side, n).wait_recv()
        for side, at in ((1, 2), (0, 3)):
            @pl.when(j == at)
            def _():
                for t in range(4):
                    yhalo(t, side).wait_recv()

        @pl.when(j == 2)
        def _():
            for side in range(2):
                xhalo(side).wait_recv()

            @pl.loop(0, NY // 8)
            def _(t):
                rows = pl.ds(pl.multiple_of(8 * t, 8), 8)
                beyond = jnp.where(lax.rem(lane, 4) >= 2, xr[0, rows, :], xr[1, rows, :])
                for z in range(CZ):
                    buf[z + 2, 4, pl.ds(pl.multiple_of(8 * t + 8, 8), 8), :] = pltpu.roll(beyond, 128 - 4 * z, 1) if z else beyond

        @pl.loop(0, 4)
        def _(q):
            strip(j, q)

        for k in range(1, NB):
            part(j, k).start()

    pl.loop(0, 2 * GROUPS)(blend)

    @pl.loop(0, 2 * GROUPS)
    def _(j):
        for k in range(1, NB):
            part(j, k).wait_send()
        for side in range(2):
            for n in range(2):
                zhalo(j // GROUPS, lax.rem(j, GROUPS), side, n).wait_send()

    for side in range(2):
        xhalo(side).wait_send()
        for t in range(4):
            yhalo(t, side).wait_send()

    @pl.loop(0, 2 * GROUPS)
    def _(j):
        for k in range(1, NB):
            final(j, k, d).wait_send()
            final(j, k, lax.rem(d + NB - k, NB)).wait_recv()

    for p in range(2):
        for n in range(2):
            o_ref[0, :, pl.ds(128 * TILES[p][n], 128)] = fbuf[2 * p + n]


def per_device(field, view_order):
    dma = pltpu.SemaphoreType.DMA
    vmem = lambda *shape: pltpu.VMEM(shape, jnp.float32)
    return pl.pallas_call(
        kernel,
        out_shape=jax.ShapeDtypeStruct((1, NY, NX), jnp.float32),
        in_specs=[pl.BlockSpec(memory_space=pltpu.HBM), pl.BlockSpec(memory_space=pltpu.HBM)],
        out_specs=pl.BlockSpec(memory_space=pltpu.VMEM),
        scratch_shapes=[
            pltpu.SMEM((NB,), jnp.int32),
            vmem(CZ + 4, 5, NY + 16, 128),
            vmem(NY, 128), vmem(2, NY, 128),
            vmem(8, 4, 8, 8, 128), vmem(8, 3, 8, 8, 128),
            vmem(8, 4, 2, 8, 128), vmem(4, NY, 128),
            dma, dma((4, 4)), dma((2, 4, 2, 2)), dma((2, 4, 2, 2)), dma((4, 2)), dma((4, 2)),
            dma((2,)), dma((2,)), dma((8, 3)), dma((8, 3)), dma((8, 3)), dma((8, 3)),
        ],
        compiler_params=pltpu.CompilerParams(
            collective_id=0, has_side_effects=True, vmem_limit_bytes=48 << 20),
    )(pltpu.with_memory_space_constraint(view_order, pltpu.HBM), field)


def solution(mesh):
    return jax.shard_map(
        per_device, mesh=mesh, in_specs=(P("depth", "row", "col"), P()),
        out_specs=P("depth", "row", "col"), check_vma=False)
```

```python
import math

import jax
import jax.numpy as jnp
from jax import lax
from jax.experimental import pallas as pl
from jax.experimental.pallas import tpu as pltpu
from jax.sharding import PartitionSpec as P

MESH = pl.DeviceIdType.MESH
CZ, NY, NX = 32, 128, 512
NB = 4
GROUPS = 4
STEP = 32
TILES = ((1, 2), (0, 3))
KEXP = -1.5 * 2.0 / 128.0 * math.log2(math.e)
BIAS = 0.3 / 0.448
SCALE = 2.0 * 0.448


def kernel(order_ref, f_ref, o_ref, vo_ref, answer, whole, beside, buf, xs, xr, stage, recv, fin, fbuf,
           vs, ld, zss, zrs, yss, yrs, xss, xrs, ass, ars, fss, frs):
    d, r, c = lax.axis_index("depth"), lax.axis_index("row"), lax.axis_index("col")
    brick = lambda k: (lax.rem(d + k, NB), r, c)
    row_to = (lax.rem(r + 1, 16), lax.rem(r + 15, 16))
    col_to = (lax.rem(c + 1, 4), lax.rem(c + 3, 4))
    lane = lax.broadcasted_iota(jnp.int32, (8, 128), 1)

    def pass_of(j):
        return lax.rem(j // 2, 2)

    def group_of(j):
        return jnp.where(j < GROUPS, 1 + lax.rem(j, 2), 3 - 3 * lax.rem(j, 2))

    def tile_of(j, n):
        return jnp.where(pass_of(j) == 0, n + 1, 3 * n)

    barrier = pltpu.get_barrier_semaphore()
    others = [(d, row_to[0], c), (d, row_to[1], c), (d, r, col_to[0]), (d, r, col_to[1])]
    odd = lax.rem(d, 2) == 1

    @pl.when(odd)
    def _():
        for k in (1, 3):
            pl.semaphore_signal(barrier, inc=1, device_id=brick(k), device_id_type=MESH)

    def load(t, g):
        return pltpu.make_async_copy(
            f_ref.at[:, pl.ds(32 * g, 32), pl.ds(128 * t, 128)],
            buf.at[pl.ds(2, CZ), t, pl.ds(8 + 32 * g, 32), :], ld.at[t, g])

    def zhalo(j, side, n):
        t, g = tile_of(j, n), group_of(j)
        src, dst, k = ((CZ - 2, 0, 1), (0, CZ + 2, 3))[side]
        return pltpu.make_async_remote_copy(
            f_ref.at[pl.ds(src, 2), pl.ds(32 * g, 32), pl.ds(128 * t, 128)],
            buf.at[pl.ds(dst, 2), t, pl.ds(8 + 32 * g, 32), :],
            zss.at[j, side, n], zrs.at[j, side, n],
            device_id=brick(k), device_id_type=MESH)

    def yhalo(t, side):
        src, dst = ((NY - 2, 6), (0, NY + 8))[side]
        return pltpu.make_async_remote_copy(
            f_ref.at[:, pl.ds(src, 2), pl.ds(128 * t, 128)],
            buf.at[pl.ds(2, CZ), t, pl.ds(dst, 2), :],
            yss.at[t, side], yrs.at[t, side],
            device_id=(d, row_to[side], c), device_id_type=MESH)

    def xhalo(side):
        return pltpu.make_async_remote_copy(
            xs, xr.at[side], xss.at[side], xrs.at[side],
            device_id=(d, r, col_to[side]), device_id_type=MESH)

    def part(j, k):
        return pltpu.make_async_remote_copy(
            stage.at[j, lax.rem(d + k, NB)], recv.at[j, k - 1],
            ass.at[j, k - 1], ars.at[j, k - 1],
            device_id=brick(k), device_id_type=MESH)

    def final(j, k, owner):
        p, g = pass_of(j), group_of(j)
        return pltpu.make_async_remote_copy(
            fin.at[j, lax.rem(d + k, NB)],
            fbuf.at[pl.ds(2 * p, 2), pl.ds(32 * g + 8 * owner, 8), :],
            fss.at[j, k - 1], frs.at[j, k - 1],
            device_id=brick(k), device_id_type=MESH)

    for t in (0, 3, 1, 2):
        for g in range(GROUPS):
            load(t, g).start(priority=1)

    order = pltpu.make_async_copy(order_ref, vo_ref, vs)
    order.start()

    @pl.when(jnp.logical_not(odd))
    def _():
        pl.semaphore_wait(barrier, 2)
        for k in (1, 3):
            pl.semaphore_signal(answer, inc=1, device_id=brick(k), device_id_type=MESH)

    @pl.when(odd)
    def _():
        pl.semaphore_wait(answer, 2)
        for dev in others:
            pl.semaphore_signal(barrier, inc=1, device_id=dev, device_id_type=MESH)
        for k in (1, 3):
            pl.semaphore_signal(whole, inc=1, device_id=brick(k), device_id_type=MESH)


    def send_zhalo(j):
        for n in range(2):
            for side in range(2):
                zhalo(j, side, n).start()

    pl.loop(0, 2 * GROUPS)(send_zhalo)

    for t in (0, 3):
        for g in range(GROUPS):
            load(t, g).wait()

    @pl.loop(0, NY // 8, unroll=2)
    def _(t):
        rows = pl.ds(pl.multiple_of(8 + 8 * t, 8), 8)
        faces = jnp.zeros((8, 128), jnp.float32)
        for z in range(CZ):
            ends = jnp.where(lane < 64, buf[2 + z, 0, rows, :], buf[2 + z, 3, rows, :])
            ends = pltpu.roll(ends, 4 * z, 1) if z else ends
            faces = jnp.where(lax.rem(lane + 2, 128) // 4 == z, ends, faces)
        xs[pl.ds(pl.multiple_of(8 * t, 8), 8), :] = faces

    for t in (1, 2):
        for g in range(GROUPS):
            load(t, g).wait()

    def strip(j, q):
        g = group_of(j)
        row = pl.multiple_of(8 + 32 * g + 8 * q, 8)
        rows = pl.ds(row, 8)
        tiles = tile_of(j, 0), tile_of(j, 1)

        def body(zz, carry):
            z0 = zz * STEP
            state = list(carry)
            for n, t in enumerate(tiles):
                col = [buf[z0 + m, t, rows, :] for m in range(STEP + 4)]
                for m in range(STEP):
                    z = z0 + m
                    energy, wsum, rsum, bsum = state[4 * n:4 * n + 4]
                    s = col[m + 2]
                    gz = 8.0 * (col[m + 3] - col[m + 1]) - (col[m + 4] - col[m])
                    yv = lambda o: buf[z + 2, t, pl.ds(row + o, 8), :]
                    gy = 8.0 * (yv(1) - yv(-1)) - (yv(2) - yv(-2))
                    prv, nxt = buf[z + 2, lax.rem(t + 4, 5), rows, :], buf[z + 2, t + 1, rows, :]
                    xp1 = pltpu.roll(jnp.where(lane < 1, nxt, s), 127, 1)
                    xp2 = pltpu.roll(jnp.where(lane < 2, nxt, s), 126, 1)
                    xm1 = pltpu.roll(jnp.where(lane >= 127, prv, s), 1, 1)
                    xm2 = pltpu.roll(jnp.where(lane >= 126, prv, s), 2, 1)
                    gx = 8.0 * (xp1 - xm1) - (xp2 - xm2)
                    norm = (gz * gz + gy * gy) + (gx * gx + 144.0)
                    along = (0.75 * gz + 0.9375 * gy) + gx
                    shade = jnp.abs(along) * lax.rsqrt(norm) + BIAS
                    recip = pl.reciprocal(1.0 + s)
                    bright = 1.0 - recip
                    after = energy * jnp.exp2(bright * KEXP)
                    weight = (energy - after) * shade
                    red = weight * bright
                    state[4 * n:4 * n + 4] = [after, wsum + weight, rsum + red, bsum + red * recip]
            return tuple(state)

        one, zero = jnp.ones((8, 128), jnp.float32), jnp.zeros((8, 128), jnp.float32)
        state = lax.fori_loop(0, CZ // STEP, body, (one, zero, zero, zero) * 2)
        for n in range(2):
            energy, wsum, rsum, bsum = state[4 * n:4 * n + 4]
            stage[j, q, 0 + n] = SCALE * rsum
            stage[j, q, 2 + n] = SCALE * (wsum - rsum)
            stage[j, q, 4 + n] = 4.0 * SCALE * bsum
            stage[j, q, 6 + n] = energy

    order.wait()
    ranks = []
    for k in range(NB):
        b = lax.rem(d + NB - k, NB)
        rank = jnp.int32(0)
        for pos in range(1, NB):
            rank = rank + jnp.where(vo_ref[pos] == b, jnp.int32(pos), jnp.int32(0))
        ranks.append(jnp.full((8, 128), rank, jnp.int32))
    ahead = [[None if e == k else ranks[e] < ranks[k] for e in range(NB)] for k in range(NB)]

    def blend(j):
        g = group_of(j)
        for k in range(1, NB):
            part(j, k).wait_recv()
        for n in range(2):
            get = lambda k, ch: stage[j, d, 2 * ch + n] if k == 0 else recv[j, k - 1, 2 * ch + n]
            through = [get(k, 3) for k in range(NB)]
            total = [jnp.zeros((8, 128), jnp.float32)] * 4
            for k in range(NB):
                factor = jnp.ones((8, 128), jnp.float32)
                for e in range(NB):
                    if e != k:
                        factor = factor * jnp.where(ahead[k][e], through[e], 1.0)
                for ch in range(3):
                    total[ch] = total[ch] + factor * get(k, ch)
                total[3] = total[3] + factor * (1.0 - through[k])
            for ch in range(4):
                fin[j, ch, n] = total[ch]
        for k in range(1, NB):
            final(j, k, d).start()
        fbuf[pl.ds(2 * pass_of(j), 2), pl.ds(pl.multiple_of(32 * g + 8 * d, 8), 8), :] = fin[j, d]

    @pl.when(jnp.logical_not(odd))
    def _():
        pl.semaphore_wait(whole, 2)

    @pl.loop(0, 2 * GROUPS)
    def _(j):
        for side in range(2):
            for n in range(2):
                zhalo(j, side, n).wait_recv()
        @pl.when(j == 0)
        def _():
            @pl.when(odd)
            def _():
                pl.semaphore_wait(barrier, len(others))
                for k in (1, 3):
                    pl.semaphore_signal(beside, inc=1, device_id=brick(k), device_id_type=MESH)

            @pl.when(jnp.logical_not(odd))
            def _():
                pl.semaphore_wait(beside, 2)

            for side in range(2):
                xhalo(side).start()
            for side in (1, 0):
                for t in range(4):
                    yhalo(t, side).start()

        for side, at in ((1, 4), (0, 5)):
            @pl.when(j == at)
            def _():
                for t in range(4):
                    yhalo(t, side).wait_recv()

        @pl.when(j == 2)
        def _():
            for side in range(2):
                xhalo(side).wait_recv()

            @pl.loop(0, NY // 8)
            def _(t):
                rows = pl.ds(pl.multiple_of(8 * t, 8), 8)
                beyond = jnp.where(lax.rem(lane, 4) >= 2, xr[0, rows, :], xr[1, rows, :])
                for z in range(CZ):
                    buf[z + 2, 4, pl.ds(pl.multiple_of(8 * t + 8, 8), 8), :] = pltpu.roll(beyond, 128 - 4 * z, 1) if z else beyond

        @pl.loop(0, 4)
        def _(q):
            strip(j, q)

        for k in range(1, NB):
            part(j, k).start()

    pl.loop(0, 2 * GROUPS)(blend)

    @pl.loop(0, 2 * GROUPS)
    def _(j):
        for k in range(1, NB):
            part(j, k).wait_send()
        for side in range(2):
            for n in range(2):
                zhalo(j, side, n).wait_send()

    for side in range(2):
        xhalo(side).wait_send()
        for t in range(4):
            yhalo(t, side).wait_send()

    @pl.loop(0, 2 * GROUPS)
    def _(j):
        for k in range(1, NB):
            final(j, k, d).wait_send()
            final(j, k, lax.rem(d + NB - k, NB)).wait_recv()

    for p in range(2):
        for n in range(2):
            o_ref[0, :, pl.ds(128 * TILES[p][n], 128)] = fbuf[2 * p + n]


def per_device(field, view_order):
    dma = pltpu.SemaphoreType.DMA
    vmem = lambda *shape: pltpu.VMEM(shape, jnp.float32)
    return pl.pallas_call(
        kernel,
        out_shape=jax.ShapeDtypeStruct((1, NY, NX), jnp.float32),
        in_specs=[pl.BlockSpec(memory_space=pltpu.HBM), pl.BlockSpec(memory_space=pltpu.HBM)],
        out_specs=pl.BlockSpec(memory_space=pltpu.VMEM),
        scratch_shapes=[
            pltpu.SMEM((NB,), jnp.int32),
            pltpu.SemaphoreType.REGULAR, pltpu.SemaphoreType.REGULAR, pltpu.SemaphoreType.REGULAR,
            vmem(CZ + 4, 5, NY + 16, 128),
            vmem(NY, 128), vmem(2, NY, 128),
            vmem(8, 4, 8, 8, 128), vmem(8, 3, 8, 8, 128),
            vmem(8, 4, 2, 8, 128), vmem(4, NY, 128),
            dma, dma((4, 4)), dma((8, 2, 2)), dma((8, 2, 2)), dma((4, 2)), dma((4, 2)),
            dma((2,)), dma((2,)), dma((8, 3)), dma((8, 3)), dma((8, 3)), dma((8, 3)),
        ],
        compiler_params=pltpu.CompilerParams(
            collective_id=0, has_side_effects=True, vmem_limit_bytes=48 << 20),
    )(pltpu.with_memory_space_constraint(view_order, pltpu.HBM), field)


def solution(mesh):
    return jax.shard_map(
        per_device, mesh=mesh, in_specs=(P("depth", "row", "col"), P()),
        out_specs=P("depth", "row", "col"), check_vma=False)
```

```python
import math

import jax
import jax.numpy as jnp
from jax import lax
from jax.experimental import pallas as pl
from jax.experimental.pallas import tpu as pltpu
from jax.sharding import PartitionSpec as P

MESH = pl.DeviceIdType.MESH
CZ, NY, NX = 32, 128, 512
NB = 4
GROUPS = 4
HOLD = 2
STEP = 32
TILES = ((1, 2), (0, 3))
KEXP = -1.5 * 2.0 / 128.0 * math.log2(math.e)
BIAS = 0.3 / 0.448
SCALE = 2.0 * 0.448


def kernel(order_ref, f_ref, o_ref, vo_ref, answer, whole, beside, buf, xs, xr, stage, recv, fin, fbuf,
           vs, ld, zss, zrs, yss, yrs, xss, xrs, ass, ars, fss, frs):
    d, r, c = lax.axis_index("depth"), lax.axis_index("row"), lax.axis_index("col")
    brick = lambda k: (lax.rem(d + k, NB), r, c)
    row_to = (lax.rem(r + 1, 16), lax.rem(r + 15, 16))
    col_to = (lax.rem(c + 1, 4), lax.rem(c + 3, 4))
    lane = lax.broadcasted_iota(jnp.int32, (8, 128), 1)

    def pass_of(j):
        return lax.rem(j // 2, 2)

    def group_of(j):
        return jnp.where(j < GROUPS, 1 + lax.rem(j, 2), 3 - 3 * lax.rem(j, 2))

    def tile_of(j, n):
        return jnp.where(pass_of(j) == 0, n + 1, 3 * n)

    barrier = pltpu.get_barrier_semaphore()
    others = [(d, row_to[0], c), (d, row_to[1], c), (d, r, col_to[0]), (d, r, col_to[1])]
    odd = lax.rem(d, 2) == 1
    second = lax.rem(r, 2) == 1

    @pl.when(odd)
    def _():
        for k in (1, 3):
            pl.semaphore_signal(barrier, inc=1, device_id=brick(k), device_id_type=MESH)

    def load(t, g):
        return pltpu.make_async_copy(
            f_ref.at[:, pl.ds(32 * g, 32), pl.ds(128 * t, 128)],
            buf.at[pl.ds(2, CZ), t, pl.ds(8 + 32 * g, 32), :], ld.at[t, g])

    def zhalo(j, side, n):
        t, g = tile_of(j, n), group_of(j)
        src, dst, k = ((CZ - 2, 0, 1), (0, CZ + 2, 3))[side]
        return pltpu.make_async_remote_copy(
            f_ref.at[pl.ds(src, 2), pl.ds(32 * g, 32), pl.ds(128 * t, 128)],
            buf.at[pl.ds(dst, 2), t, pl.ds(8 + 32 * g, 32), :],
            zss.at[j, side, n], zrs.at[j, side, n],
            device_id=brick(k), device_id_type=MESH)

    def yhalo(t, side):
        src, dst = ((NY - 2, 6), (0, NY + 8))[side]
        return pltpu.make_async_remote_copy(
            f_ref.at[:, pl.ds(src, 2), pl.ds(128 * t, 128)],
            buf.at[pl.ds(2, CZ), t, pl.ds(dst, 2), :],
            yss.at[t, side], yrs.at[t, side],
            device_id=(d, row_to[side], c), device_id_type=MESH)

    def xhalo(side):
        return pltpu.make_async_remote_copy(
            xs, xr.at[side], xss.at[side], xrs.at[side],
            device_id=(d, r, col_to[side]), device_id_type=MESH)

    def part(j, k):
        return pltpu.make_async_remote_copy(
            stage.at[j, lax.rem(d + k, NB)], recv.at[j, k - 1],
            ass.at[j, k - 1], ars.at[j, k - 1],
            device_id=brick(k), device_id_type=MESH)

    def final(j, k, owner):
        p, g = pass_of(j), group_of(j)
        return pltpu.make_async_remote_copy(
            fin.at[j, lax.rem(d + k, NB)],
            fbuf.at[pl.ds(2 * p, 2), pl.ds(32 * g + 8 * owner, 8), :],
            fss.at[j, k - 1], frs.at[j, k - 1],
            device_id=brick(k), device_id_type=MESH)

    for t in (0, 3, 1, 2):
        for g in range(GROUPS):
            load(t, g).start(priority=1)

    order = pltpu.make_async_copy(order_ref, vo_ref, vs)
    order.start()

    @pl.when(jnp.logical_not(odd))
    def _():
        pl.semaphore_wait(barrier, 2)
        for k in (1, 3):
            pl.semaphore_signal(answer, inc=1, device_id=brick(k), device_id_type=MESH)

    @pl.when(odd)
    def _():
        pl.semaphore_wait(answer, 2)
        for dev in others:
            pl.semaphore_signal(barrier, inc=1, device_id=dev, device_id_type=MESH)
        for k in (1, 3):
            pl.semaphore_signal(whole, inc=1, device_id=brick(k), device_id_type=MESH)


    def send_zhalo(j):
        for n in range(2):
            for side in range(2):
                zhalo(j, side, n).start()

    pl.loop(0, 2 * GROUPS)(send_zhalo)

    for t in (0, 3):
        for g in range(GROUPS):
            load(t, g).wait()

    @pl.loop(0, NY // 8, unroll=2)
    def _(t):
        rows = pl.ds(pl.multiple_of(8 + 8 * t, 8), 8)
        faces = jnp.zeros((8, 128), jnp.float32)
        for z in range(CZ):
            ends = jnp.where(lane < 64, buf[2 + z, 0, rows, :], buf[2 + z, 3, rows, :])
            ends = pltpu.roll(ends, 4 * z, 1) if z else ends
            faces = jnp.where(lax.rem(lane + 2, 128) // 4 == z, ends, faces)
        xs[pl.ds(pl.multiple_of(8 * t, 8), 8), :] = faces

    for t in (1, 2):
        for g in range(GROUPS):
            load(t, g).wait()

    def strip(j, q):
        g = group_of(j)
        row = pl.multiple_of(8 + 32 * g + 8 * q, 8)
        rows = pl.ds(row, 8)
        tiles = tile_of(j, 0), tile_of(j, 1)

        def body(zz, carry):
            z0 = zz * STEP
            state = list(carry)
            for n, t in enumerate(tiles):
                col = [buf[z0 + m, t, rows, :] for m in range(STEP + 4)]
                for m in range(STEP):
                    z = z0 + m
                    energy, wsum, rsum, bsum = state[4 * n:4 * n + 4]
                    s = col[m + 2]
                    gz = 8.0 * (col[m + 3] - col[m + 1]) - (col[m + 4] - col[m])
                    yv = lambda o: buf[z + 2, t, pl.ds(row + o, 8), :]
                    gy = 8.0 * (yv(1) - yv(-1)) - (yv(2) - yv(-2))
                    prv, nxt = buf[z + 2, lax.rem(t + 4, 5), rows, :], buf[z + 2, t + 1, rows, :]
                    xp1 = pltpu.roll(jnp.where(lane < 1, nxt, s), 127, 1)
                    xp2 = pltpu.roll(jnp.where(lane < 2, nxt, s), 126, 1)
                    xm1 = pltpu.roll(jnp.where(lane >= 127, prv, s), 1, 1)
                    xm2 = pltpu.roll(jnp.where(lane >= 126, prv, s), 2, 1)
                    gx = 8.0 * (xp1 - xm1) - (xp2 - xm2)
                    norm = (gz * gz + gy * gy) + (gx * gx + 144.0)
                    along = (0.75 * gz + 0.9375 * gy) + gx
                    shade = jnp.abs(along) * lax.rsqrt(norm) + BIAS
                    recip = pl.reciprocal(1.0 + s)
                    bright = 1.0 - recip
                    after = energy * jnp.exp2(bright * KEXP)
                    weight = (energy - after) * shade
                    red = weight * bright
                    state[4 * n:4 * n + 4] = [after, wsum + weight, rsum + red, bsum + red * recip]
            return tuple(state)

        one, zero = jnp.ones((8, 128), jnp.float32), jnp.zeros((8, 128), jnp.float32)
        state = lax.fori_loop(0, CZ // STEP, body, (one, zero, zero, zero) * 2)
        for n in range(2):
            energy, wsum, rsum, bsum = state[4 * n:4 * n + 4]
            stage[j, q, 0 + n] = SCALE * rsum
            stage[j, q, 2 + n] = SCALE * (wsum - rsum)
            stage[j, q, 4 + n] = 4.0 * SCALE * bsum
            stage[j, q, 6 + n] = energy

    order.wait()
    ranks = []
    for k in range(NB):
        b = lax.rem(d + NB - k, NB)
        rank = jnp.int32(0)
        for pos in range(1, NB):
            rank = rank + jnp.where(vo_ref[pos] == b, jnp.int32(pos), jnp.int32(0))
        ranks.append(jnp.full((8, 128), rank, jnp.int32))
    ahead = [[None if e == k else ranks[e] < ranks[k] for e in range(NB)] for k in range(NB)]

    def blend(j):
        g = group_of(j)
        for k in range(1, NB):
            part(j, k).wait_recv()
        for n in range(2):
            get = lambda k, ch: stage[j, d, 2 * ch + n] if k == 0 else recv[j, k - 1, 2 * ch + n]
            through = [get(k, 3) for k in range(NB)]
            total = [jnp.zeros((8, 128), jnp.float32)] * 4
            for k in range(NB):
                factor = jnp.ones((8, 128), jnp.float32)
                for e in range(NB):
                    if e != k:
                        factor = factor * jnp.where(ahead[k][e], through[e], 1.0)
                for ch in range(3):
                    total[ch] = total[ch] + factor * get(k, ch)
                total[3] = total[3] + factor * (1.0 - through[k])
            for ch in range(4):
                fin[j, ch, n] = total[ch]
        for k in range(1, NB):
            final(j, k, d).start()
        fbuf[pl.ds(2 * pass_of(j), 2), pl.ds(pl.multiple_of(32 * g + 8 * d, 8), 8), :] = fin[j, d]

    @pl.when(jnp.logical_not(odd))
    def _():
        pl.semaphore_wait(whole, 2)

    @pl.loop(0, 2 * GROUPS)
    def _(j):
        for side in range(2):
            for n in range(2):
                zhalo(j, side, n).wait_recv()
        @pl.when(j == 0)
        def _():
            @pl.when(odd)
            def _():
                pl.semaphore_wait(barrier, len(others))
                for k in (1, 3):
                    pl.semaphore_signal(beside, inc=1, device_id=brick(k), device_id_type=MESH)

            @pl.when(jnp.logical_not(odd))
            def _():
                pl.semaphore_wait(beside, 2)

            for side in range(2):
                xhalo(side).start()
            for side in (1, 0):
                for t in range(4):
                    yhalo(t, side).start()

        for side, at in ((1, 4), (0, 5)):
            @pl.when(j == at)
            def _():
                for t in range(4):
                    yhalo(t, side).wait_recv()

        @pl.when(j == 2)
        def _():
            for side in range(2):
                xhalo(side).wait_recv()

            @pl.loop(0, NY // 8)
            def _(t):
                rows = pl.ds(pl.multiple_of(8 * t, 8), 8)
                beyond = jnp.where(lax.rem(lane, 4) >= 2, xr[0, rows, :], xr[1, rows, :])
                for z in range(CZ):
                    buf[z + 2, 4, pl.ds(pl.multiple_of(8 * t + 8, 8), 8), :] = pltpu.roll(beyond, 128 - 4 * z, 1) if z else beyond

        @pl.loop(0, 4)
        def _(q):
            strip(j, q)

        @pl.when(jnp.logical_not(second))
        def _():
            for k in range(1, NB):
                part(j, k).start()

        @pl.when(jnp.logical_and(second, j >= HOLD))
        def _():
            for k in range(1, NB):
                part(j - HOLD, k).start()

    @pl.when(second)
    def _():
        @pl.loop(2 * GROUPS - HOLD, 2 * GROUPS)
        def _(j):
            for k in range(1, NB):
                part(j, k).start()

    pl.loop(0, 2 * GROUPS)(blend)

    @pl.loop(0, 2 * GROUPS)
    def _(j):
        for k in range(1, NB):
            part(j, k).wait_send()
        for side in range(2):
            for n in range(2):
                zhalo(j, side, n).wait_send()

    for side in range(2):
        xhalo(side).wait_send()
        for t in range(4):
            yhalo(t, side).wait_send()

    @pl.loop(0, 2 * GROUPS)
    def _(j):
        for k in range(1, NB):
            final(j, k, d).wait_send()
            final(j, k, lax.rem(d + NB - k, NB)).wait_recv()

    for p in range(2):
        for n in range(2):
            o_ref[0, :, pl.ds(128 * TILES[p][n], 128)] = fbuf[2 * p + n]


def per_device(field, view_order):
    dma = pltpu.SemaphoreType.DMA
    vmem = lambda *shape: pltpu.VMEM(shape, jnp.float32)
    return pl.pallas_call(
        kernel,
        out_shape=jax.ShapeDtypeStruct((1, NY, NX), jnp.float32),
        in_specs=[pl.BlockSpec(memory_space=pltpu.HBM), pl.BlockSpec(memory_space=pltpu.HBM)],
        out_specs=pl.BlockSpec(memory_space=pltpu.VMEM),
        scratch_shapes=[
            pltpu.SMEM((NB,), jnp.int32),
            pltpu.SemaphoreType.REGULAR, pltpu.SemaphoreType.REGULAR, pltpu.SemaphoreType.REGULAR,
            vmem(CZ + 4, 5, NY + 16, 128),
            vmem(NY, 128), vmem(2, NY, 128),
            vmem(8, 4, 8, 8, 128), vmem(8, 3, 8, 8, 128),
            vmem(8, 4, 2, 8, 128), vmem(4, NY, 128),
            dma, dma((4, 4)), dma((8, 2, 2)), dma((8, 2, 2)), dma((4, 2)), dma((4, 2)),
            dma((2,)), dma((2,)), dma((8, 3)), dma((8, 3)), dma((8, 3)), dma((8, 3)),
        ],
        compiler_params=pltpu.CompilerParams(
            collective_id=0, has_side_effects=True, vmem_limit_bytes=48 << 20),
    )(pltpu.with_memory_space_constraint(view_order, pltpu.HBM), field)


def solution(mesh):
    return jax.shard_map(
        per_device, mesh=mesh, in_specs=(P("depth", "row", "col"), P()),
        out_specs=P("depth", "row", "col"), check_vma=False)
```

```python
import math

import jax
import jax.numpy as jnp
from jax import lax
from jax.experimental import pallas as pl
from jax.experimental.pallas import tpu as pltpu
from jax.sharding import PartitionSpec as P

MESH = pl.DeviceIdType.MESH
CZ, NY, NX = 32, 128, 512
NB = 4
GROUPS = 4
LEAD = 3
STEP = 32
TILES = ((1, 2), (0, 3))
KEXP = -1.5 * 2.0 / 128.0 * math.log2(math.e)
BIAS = 0.3 / 0.448
SCALE = 2.0 * 0.448


def kernel(order_ref, f_ref, o_ref, vo_ref, answer, whole, beside, buf, xs, xr, stage, recv, fin, fbuf,
           vs, ld, zss, zrs, yss, yrs, xss, xrs, ass, ars, fss, frs):
    d, r, c = lax.axis_index("depth"), lax.axis_index("row"), lax.axis_index("col")
    brick = lambda k: (lax.rem(d + k, NB), r, c)
    row_to = (lax.rem(r + 1, 16), lax.rem(r + 15, 16))
    col_to = (lax.rem(c + 1, 4), lax.rem(c + 3, 4))
    lane = lax.broadcasted_iota(jnp.int32, (8, 128), 1)

    def pass_of(j):
        return lax.rem(j // 2, 2)

    def group_of(j):
        return jnp.where(j < GROUPS, 1 + lax.rem(j, 2), 3 - 3 * lax.rem(j, 2))

    def tile_of(j, n):
        return jnp.where(pass_of(j) == 0, n + 1, 3 * n)

    barrier = pltpu.get_barrier_semaphore()
    others = [(d, row_to[0], c), (d, row_to[1], c), (d, r, col_to[0]), (d, r, col_to[1])]
    odd = lax.rem(d, 2) == 1

    @pl.when(odd)
    def _():
        for k in (1, 3):
            pl.semaphore_signal(barrier, inc=1, device_id=brick(k), device_id_type=MESH)

    def load(t, g):
        return pltpu.make_async_copy(
            f_ref.at[:, pl.ds(32 * g, 32), pl.ds(128 * t, 128)],
            buf.at[pl.ds(2, CZ), t, pl.ds(8 + 32 * g, 32), :], ld.at[t, g])

    def zhalo(j, side, n):
        t, g = tile_of(j, n), group_of(j)
        src, dst, k = ((CZ - 2, 0, 1), (0, CZ + 2, 3))[side]
        return pltpu.make_async_remote_copy(
            f_ref.at[pl.ds(src, 2), pl.ds(32 * g, 32), pl.ds(128 * t, 128)],
            buf.at[pl.ds(dst, 2), t, pl.ds(8 + 32 * g, 32), :],
            zss.at[j, side, n], zrs.at[j, side, n],
            device_id=brick(k), device_id_type=MESH)

    def yhalo(t, side):
        src, dst = ((NY - 2, 6), (0, NY + 8))[side]
        return pltpu.make_async_remote_copy(
            f_ref.at[:, pl.ds(src, 2), pl.ds(128 * t, 128)],
            buf.at[pl.ds(2, CZ), t, pl.ds(dst, 2), :],
            yss.at[t, side], yrs.at[t, side],
            device_id=(d, row_to[side], c), device_id_type=MESH)

    def xhalo(side):
        return pltpu.make_async_remote_copy(
            xs, xr.at[side], xss.at[side], xrs.at[side],
            device_id=(d, r, col_to[side]), device_id_type=MESH)

    def part(j, k):
        return pltpu.make_async_remote_copy(
            stage.at[j, lax.rem(d + k, NB)], recv.at[j, k - 1],
            ass.at[j, k - 1], ars.at[j, k - 1],
            device_id=brick(k), device_id_type=MESH)

    def final(j, k, owner):
        p, g = pass_of(j), group_of(j)
        return pltpu.make_async_remote_copy(
            fin.at[j, lax.rem(d + k, NB)],
            fbuf.at[pl.ds(2 * p, 2), pl.ds(32 * g + 8 * owner, 8), :],
            fss.at[j, k - 1], frs.at[j, k - 1],
            device_id=brick(k), device_id_type=MESH)

    for t in (0, 3, 1, 2):
        for g in range(GROUPS):
            load(t, g).start(priority=1)

    order = pltpu.make_async_copy(order_ref, vo_ref, vs)
    order.start()

    @pl.when(jnp.logical_not(odd))
    def _():
        pl.semaphore_wait(barrier, 2)
        for k in (1, 3):
            pl.semaphore_signal(answer, inc=1, device_id=brick(k), device_id_type=MESH)

    @pl.when(odd)
    def _():
        pl.semaphore_wait(answer, 2)
        for dev in others:
            pl.semaphore_signal(barrier, inc=1, device_id=dev, device_id_type=MESH)
        for k in (1, 3):
            pl.semaphore_signal(whole, inc=1, device_id=brick(k), device_id_type=MESH)


    def send_zhalo(j):
        for n in range(2):
            for side in range(2):
                zhalo(j, side, n).start()

    second = lax.rem(r, 2) == 1
    pl.loop(0, LEAD)(send_zhalo)

    @pl.when(jnp.logical_not(second))
    def _():
        pl.loop(LEAD, 2 * GROUPS)(send_zhalo)


    for t in (0, 3):
        for g in range(GROUPS):
            load(t, g).wait()

    @pl.loop(0, NY // 8, unroll=2)
    def _(t):
        rows = pl.ds(pl.multiple_of(8 + 8 * t, 8), 8)
        faces = jnp.zeros((8, 128), jnp.float32)
        for z in range(CZ):
            ends = jnp.where(lane < 64, buf[2 + z, 0, rows, :], buf[2 + z, 3, rows, :])
            ends = pltpu.roll(ends, 4 * z, 1) if z else ends
            faces = jnp.where(lax.rem(lane + 2, 128) // 4 == z, ends, faces)
        xs[pl.ds(pl.multiple_of(8 * t, 8), 8), :] = faces

    for t in (1, 2):
        for g in range(GROUPS):
            load(t, g).wait()

    def strip(j, q):
        g = group_of(j)
        row = pl.multiple_of(8 + 32 * g + 8 * q, 8)
        rows = pl.ds(row, 8)
        tiles = tile_of(j, 0), tile_of(j, 1)

        def body(zz, carry):
            z0 = zz * STEP
            state = list(carry)
            for n, t in enumerate(tiles):
                col = [buf[z0 + m, t, rows, :] for m in range(STEP + 4)]
                for m in range(STEP):
                    z = z0 + m
                    energy, wsum, rsum, bsum = state[4 * n:4 * n + 4]
                    s = col[m + 2]
                    gz = 8.0 * (col[m + 3] - col[m + 1]) - (col[m + 4] - col[m])
                    yv = lambda o: buf[z + 2, t, pl.ds(row + o, 8), :]
                    gy = 8.0 * (yv(1) - yv(-1)) - (yv(2) - yv(-2))
                    prv, nxt = buf[z + 2, lax.rem(t + 4, 5), rows, :], buf[z + 2, t + 1, rows, :]
                    xp1 = pltpu.roll(jnp.where(lane < 1, nxt, s), 127, 1)
                    xp2 = pltpu.roll(jnp.where(lane < 2, nxt, s), 126, 1)
                    xm1 = pltpu.roll(jnp.where(lane >= 127, prv, s), 1, 1)
                    xm2 = pltpu.roll(jnp.where(lane >= 126, prv, s), 2, 1)
                    gx = 8.0 * (xp1 - xm1) - (xp2 - xm2)
                    norm = (gz * gz + gy * gy) + (gx * gx + 144.0)
                    along = (0.75 * gz + 0.9375 * gy) + gx
                    shade = jnp.abs(along) * lax.rsqrt(norm) + BIAS
                    recip = pl.reciprocal(1.0 + s)
                    bright = 1.0 - recip
                    after = energy * jnp.exp2(bright * KEXP)
                    weight = (energy - after) * shade
                    red = weight * bright
                    state[4 * n:4 * n + 4] = [after, wsum + weight, rsum + red, bsum + red * recip]
            return tuple(state)

        one, zero = jnp.ones((8, 128), jnp.float32), jnp.zeros((8, 128), jnp.float32)
        state = lax.fori_loop(0, CZ // STEP, body, (one, zero, zero, zero) * 2)
        for n in range(2):
            energy, wsum, rsum, bsum = state[4 * n:4 * n + 4]
            stage[j, q, 0 + n] = SCALE * rsum
            stage[j, q, 2 + n] = SCALE * (wsum - rsum)
            stage[j, q, 4 + n] = 4.0 * SCALE * bsum
            stage[j, q, 6 + n] = energy

    order.wait()
    ranks = []
    for k in range(NB):
        b = lax.rem(d + NB - k, NB)
        rank = jnp.int32(0)
        for pos in range(1, NB):
            rank = rank + jnp.where(vo_ref[pos] == b, jnp.int32(pos), jnp.int32(0))
        ranks.append(jnp.full((8, 128), rank, jnp.int32))
    ahead = [[None if e == k else ranks[e] < ranks[k] for e in range(NB)] for k in range(NB)]

    def blend(j):
        g = group_of(j)
        for k in range(1, NB):
            part(j, k).wait_recv()
        for n in range(2):
            get = lambda k, ch: stage[j, d, 2 * ch + n] if k == 0 else recv[j, k - 1, 2 * ch + n]
            through = [get(k, 3) for k in range(NB)]
            total = [jnp.zeros((8, 128), jnp.float32)] * 4
            for k in range(NB):
                factor = jnp.ones((8, 128), jnp.float32)
                for e in range(NB):
                    if e != k:
                        factor = factor * jnp.where(ahead[k][e], through[e], 1.0)
                for ch in range(3):
                    total[ch] = total[ch] + factor * get(k, ch)
                total[3] = total[3] + factor * (1.0 - through[k])
            for ch in range(4):
                fin[j, ch, n] = total[ch]
        for k in range(1, NB):
            final(j, k, d).start()
        fbuf[pl.ds(2 * pass_of(j), 2), pl.ds(pl.multiple_of(32 * g + 8 * d, 8), 8), :] = fin[j, d]

    @pl.when(jnp.logical_not(odd))
    def _():
        pl.semaphore_wait(whole, 2)

    @pl.loop(0, 2 * GROUPS)
    def _(j):
        @pl.when(jnp.logical_and(second, j < 2 * GROUPS - LEAD))
        def _():
            send_zhalo(j + LEAD)

        for side in range(2):
            for n in range(2):
                zhalo(j, side, n).wait_recv()
        @pl.when(j == 0)
        def _():
            @pl.when(odd)
            def _():
                pl.semaphore_wait(barrier, len(others))
                for k in (1, 3):
                    pl.semaphore_signal(beside, inc=1, device_id=brick(k), device_id_type=MESH)

            @pl.when(jnp.logical_not(odd))
            def _():
                pl.semaphore_wait(beside, 2)

            for side in range(2):
                xhalo(side).start()
            for side in (1, 0):
                for t in range(4):
                    yhalo(t, side).start()

        for side, at in ((1, 4), (0, 5)):
            @pl.when(j == at)
            def _():
                for t in range(4):
                    yhalo(t, side).wait_recv()

        @pl.when(j == 2)
        def _():
            for side in range(2):
                xhalo(side).wait_recv()

            @pl.loop(0, NY // 8)
            def _(t):
                rows = pl.ds(pl.multiple_of(8 * t, 8), 8)
                beyond = jnp.where(lax.rem(lane, 4) >= 2, xr[0, rows, :], xr[1, rows, :])
                for z in range(CZ):
                    buf[z + 2, 4, pl.ds(pl.multiple_of(8 * t + 8, 8), 8), :] = pltpu.roll(beyond, 128 - 4 * z, 1) if z else beyond

        @pl.loop(0, 4)
        def _(q):
            strip(j, q)

        for k in range(1, NB):
            part(j, k).start()

    pl.loop(0, 2 * GROUPS)(blend)

    @pl.loop(0, 2 * GROUPS)
    def _(j):
        for k in range(1, NB):
            part(j, k).wait_send()
        for side in range(2):
            for n in range(2):
                zhalo(j, side, n).wait_send()

    for side in range(2):
        xhalo(side).wait_send()
        for t in range(4):
            yhalo(t, side).wait_send()

    @pl.loop(0, 2 * GROUPS)
    def _(j):
        for k in range(1, NB):
            final(j, k, d).wait_send()
            final(j, k, lax.rem(d + NB - k, NB)).wait_recv()

    for p in range(2):
        for n in range(2):
            o_ref[0, :, pl.ds(128 * TILES[p][n], 128)] = fbuf[2 * p + n]


def per_device(field, view_order):
    dma = pltpu.SemaphoreType.DMA
    vmem = lambda *shape: pltpu.VMEM(shape, jnp.float32)
    return pl.pallas_call(
        kernel,
        out_shape=jax.ShapeDtypeStruct((1, NY, NX), jnp.float32),
        in_specs=[pl.BlockSpec(memory_space=pltpu.HBM), pl.BlockSpec(memory_space=pltpu.HBM)],
        out_specs=pl.BlockSpec(memory_space=pltpu.VMEM),
        scratch_shapes=[
            pltpu.SMEM((NB,), jnp.int32),
            pltpu.SemaphoreType.REGULAR, pltpu.SemaphoreType.REGULAR, pltpu.SemaphoreType.REGULAR,
            vmem(CZ + 4, 5, NY + 16, 128),
            vmem(NY, 128), vmem(2, NY, 128),
            vmem(8, 4, 8, 8, 128), vmem(8, 3, 8, 8, 128),
            vmem(8, 4, 2, 8, 128), vmem(4, NY, 128),
            dma, dma((4, 4)), dma((8, 2, 2)), dma((8, 2, 2)), dma((4, 2)), dma((4, 2)),
            dma((2,)), dma((2,)), dma((8, 3)), dma((8, 3)), dma((8, 3)), dma((8, 3)),
        ],
        compiler_params=pltpu.CompilerParams(
            collective_id=0, has_side_effects=True, vmem_limit_bytes=48 << 20),
    )(pltpu.with_memory_space_constraint(view_order, pltpu.HBM), field)


def solution(mesh):
    return jax.shard_map(
        per_device, mesh=mesh, in_specs=(P("depth", "row", "col"), P()),
        out_specs=P("depth", "row", "col"), check_vma=False)
```
